128 devices in a mesh: enc: 8 (over x, core), own: 16 (over z, y).
Axes of the slice: x: 4, y: 4, z: 4, core: 2. Of those that a mesh axis runs over, the one named last changes fastest.
Arguments:
- features: bfloat16 [8192, 768], P(('enc', 'own')), may hold values from -6 to 6
- doc_cluster: int32 [8192], P(('enc', 'own')), may hold values from 0 to 63, as said below
- norm_gain: float32 [768], replicated, may hold values from 0.25 to 1.75
- w_in: bfloat16 [768, 3072], replicated, may hold values from -0.21875 to 0.21875
- b_in: float32 [3072], replicated, may hold values from -3 to 3
- w_out: bfloat16 [3072, 768], replicated, may hold values from -0.109375 to 0.109375
- members: bfloat16 [16, 8192, 768], P('own', 'enc'), may hold values from -6 to 6
- member_cluster: int32 [16, 8192], P('own', 'enc'), may hold values from 0 to 63, as said below
- cluster_range: int32 [64, 2], replicated, may hold values from 0 to 15, as said below
Outputs:
- embeddings: bfloat16 [8192, 768], P(('enc', 'own'))
- maxsim: float32 [8192], P(('enc', 'own'))
The draws below stay inside these ranges and needn't reach their ends.
Inputs may be any that keep to these rules, and one draw needn't show every extreme that they name: `doc_cluster`: document k of a device's 64 belongs to a cluster whose range lies in owner group g = k mod (4), the owners 4 g to 4 g + 3. Of one device's documents at most 16 belong to clusters whose range holds a given owner; on every device some owner gets exactly 16. `cluster_range`: each cluster's range is an aligned run of 1, 2 or 4 owners inside an aligned group of four owners; every such group has a cluster that spans all four. `member_cluster`: A member's cluster has a range that holds the member's owner, and every owner in a cluster's range holds members of it.
All inputs are finite; a program needn't handle non-finite values.
Results may differ from the reference program's by a relative error of at most 0.0047.
Values may be sent and summed in bfloat16 or wider, within the bound.
A program may use at most 64 MiB of HBM per device.

```python
import math
import jax
import jax.numpy as jnp
from jax import lax

D = 768
HID = 3072
DOC_DEV = 64
CL_OWN = 4
DOCS = 8192
OWNERS = 16
RES_COL = 8192
NCLUST = 64


def span_table(key):
    index = jnp.arange(NCLUST, dtype=jnp.int32)
    power = jax.random.randint(jax.random.fold_in(key, 11), (NCLUST,), 0, 3)
    drawn = jnp.where(power == 0, 1, jnp.where(power == 1, 2, 4))
    span = jnp.where(index % (4 * CL_OWN) == 0, 4, drawn).astype(jnp.int32)
    anchor = index // CL_OWN
    lowest = anchor - anchor % span
    return (lowest.astype(jnp.int32), (lowest + span - 1).astype(jnp.int32))


def draw_cluster_range(key, part):
    lowest, highest = span_table(key)
    return jnp.stack([lowest, highest], axis=1).astype(jnp.int32)


def draw_doc_cluster(key, part):
    lowest, highest = span_table(key)
    quads = OWNERS // 4
    group = 4 * CL_OWN
    blocks = DOCS // DOC_DEV
    position = jnp.arange(DOC_DEV, dtype=jnp.int32)
    quad = position % quads
    chosen = jax.random.randint(jax.random.fold_in(key, 21), (blocks, DOC_DEV), 0, group)
    entries = quad[None, :] * group + chosen
    heated = jax.random.randint(jax.random.fold_in(key, 22), (blocks,), 0, quads)
    spanning = highest - lowest == 3
    offsets = jnp.arange(group, dtype=jnp.int32)
    candidate = quad[:, None] * group + offsets[None, :]
    allowed = spanning[candidate]
    scores = jax.random.randint(jax.random.fold_in(key, 23), (blocks, DOC_DEV, group), 0, 1 << 16) * group + offsets[None, None, :]
    winner = jnp.argmax(jnp.where(allowed[None, :, :], scores, -1), axis=-1).astype(jnp.int32)
    spread_out = quad[None, :] * group + winner
    result = jnp.where(quad[None, :] == heated[:, None], spread_out, entries)
    return result.reshape(DOCS).astype(jnp.int32)


def draw_member_cluster(key, part):
    lowest, highest = span_table(key)
    owner = jnp.arange(OWNERS, dtype=jnp.int32)
    covers = (lowest[None, :] <= owner[:, None]) & (highest[None, :] >= owner[:, None])
    flags = covers.astype(jnp.int32)
    rank = jnp.cumsum(flags, axis=1) - 1
    number = jnp.sum(flags, axis=1)
    slot = jnp.arange(RES_COL, dtype=jnp.int32)
    first = jnp.argmax((covers[:, None, :] & (rank[:, None, :] == slot[None, :, None])).astype(jnp.int32), axis=-1).astype(jnp.int32)
    labels = jnp.arange(NCLUST, dtype=jnp.int32)
    scores = jax.random.randint(jax.random.fold_in(key, 31), (OWNERS, RES_COL, NCLUST), 0, 1 << 16) * NCLUST + labels[None, None, :]
    other = jnp.argmax(jnp.where(covers[:, None, :], scores, -1), axis=-1).astype(jnp.int32)
    chosen = jnp.where(slot[None, :] < number[:, None], first, other)
    shuffle = jax.random.randint(jax.random.fold_in(key, 32), (OWNERS, RES_COL), 0, 1 << 16) * RES_COL + slot[None, :]
    order = jnp.argsort(shuffle, axis=1).astype(jnp.int32)
    return jnp.take_along_axis(chosen, order, axis=1).astype(jnp.int32)


def shard_levels(stream_key, shape, shards, low, high):
    gain, own = 1.0, jax.random.fold_in(stream_key, 6)
    for dim, parts in shards:
        heights = jnp.exp(jax.random.uniform(jax.random.fold_in(own, dim), (parts,), jnp.float32, low / len(shards), high / len(shards)))
        gain = gain * jnp.repeat(heights, shape[dim] // parts).reshape([-1 if axis == dim else 1 for axis in range(len(shape))])
    return gain


def centred(rng, extent, scale, bound, shards=(), kind=jnp.bfloat16):
    loudness = shard_levels(rng, extent, shards, -0.22, 0.18) if shards else 1.0
    entries = jax.random.normal(rng, extent, jnp.float32) * scale * loudness
    return jnp.minimum(jnp.maximum(entries, -bound), bound).astype(kind)


def setup_inputs(seed: int = 0) -> dict:
    key_of = jax.random.split(jax.random.key(seed), 10)
    features = centred(key_of[0], (DOCS, D), 1.0, 6.0, ((0, 128),))
    doc_cluster = draw_doc_cluster(jax.random.fold_in(key_of[9], 71), 0)
    norm_gain = jnp.clip(1.0 + 0.15 * jax.random.normal(key_of[2], (D,), jnp.float32), 0.25, 1.75)
    w_in = centred(key_of[3], (D, HID), D ** -0.5, 0.21875)
    b_in = centred(key_of[4], (HID,), 0.5, 3.0, (), jnp.float32)
    w_out = centred(key_of[5], (HID, D), HID ** -0.5, 0.109375)
    members = centred(key_of[6], (OWNERS, RES_COL, D), 1.0, 6.0, ((0, 16), (1, 8)))
    member_cluster = draw_member_cluster(jax.random.fold_in(key_of[9], 71), 0)
    cluster_range = draw_cluster_range(jax.random.fold_in(key_of[9], 71), 0)
    return {"features": features, "doc_cluster": doc_cluster, "norm_gain": norm_gain, "w_in": w_in, "b_in": b_in, "w_out": w_out, "members": members, "member_cluster": member_cluster, "cluster_range": cluster_range}


lowest_score = -1e+30

def encode_block(rows, norm_gain, w_in, b_in, w_out):
    inputs = rows.astype(jnp.float32)
    center = inputs - lax.optimization_barrier(jnp.mean(inputs, axis=1, keepdims=True))
    spread = lax.optimization_barrier(jnp.mean(center * center, axis=1, keepdims=True))
    normed = (center * lax.rsqrt(spread + 1e-05) * norm_gain).astype(jnp.bfloat16)
    hidden = jax.nn.gelu(jnp.dot(normed, w_in, preferred_element_type=jnp.float32) + b_in, approximate=True).astype(jnp.bfloat16)
    output = inputs + jnp.dot(hidden, w_out, preferred_element_type=jnp.float32)
    return (output * lax.rsqrt(lax.optimization_barrier(jnp.mean(output * output, axis=1, keepdims=True)) + 1e-06)).astype(jnp.bfloat16)

def best_match(rows, labels, lowest, highest, stored, stored_labels, stored_owner):
    count = rows.shape[0]
    total = stored.shape[0]
    width = rows.shape[1]
    row_block = 2048 if count % 2048 == 0 else count
    col_block = 1024 if total % 1024 == 0 else total
    scale = 1.0 / math.sqrt(width)
    stored_blocks = stored.astype(jnp.float32).reshape(total // col_block, col_block, width)
    label_blocks = stored_labels.reshape(total // col_block, col_block)
    owner_blocks = stored_owner.reshape(total // col_block, col_block)

    def one_block(group):
        block, block_labels, block_low, block_high = group
        block = block.astype(jnp.float32)

        def advance(best, pieces):
            stock, stock_labels, stock_owner = pieces
            score = jnp.dot(block, stock.T, precision=lax.Precision.HIGHEST) * scale
            inside = (block_labels[:, None] == stock_labels[None, :]) & (stock_owner[None, :] >= block_low[:, None]) & (stock_owner[None, :] <= block_high[:, None])
            score = jnp.where(inside, score, lowest_score)
            return (jnp.maximum(best, lax.optimization_barrier(jnp.max(score, axis=1))), None)
        start = jnp.full((block.shape[0],), lowest_score, jnp.float32)
        best, unused = lax.scan(advance, start, (stored_blocks, label_blocks, owner_blocks))
        return best
    result = lax.map(one_block, (rows.reshape(count // row_block, row_block, width), labels.reshape(count // row_block, row_block), lowest.reshape(count // row_block, row_block), highest.reshape(count // row_block, row_block)))
    return result.reshape(count)

def reference(features, doc_cluster, norm_gain, w_in, b_in, w_out, members, member_cluster, cluster_range):
    blocks = features.reshape(DOCS // DOC_DEV, DOC_DEV, D)
    embeddings = lax.map(lambda rows: encode_block(rows, norm_gain, w_in, b_in, w_out), blocks).reshape(DOCS, D)
    quads = OWNERS // 4
    per_block = DOC_DEV // quads
    grouped = embeddings.reshape(DOCS // DOC_DEV, per_block, quads, D).transpose(2, 0, 1, 3).reshape(quads, -1, D)
    labels = doc_cluster.reshape(DOCS // DOC_DEV, per_block, quads).transpose(2, 0, 1).reshape(quads, -1)
    lowest = cluster_range[:, 0][labels]
    highest = cluster_range[:, 1][labels]
    stored = members.reshape(quads, 4 * RES_COL, D)
    stored_labels = member_cluster.reshape(quads, 4 * RES_COL)
    owner_ids = jnp.broadcast_to(jnp.arange(OWNERS, dtype=jnp.int32)[:, None], (OWNERS, RES_COL)).reshape(quads, 4 * RES_COL)
    best = lax.map(lambda group: best_match(*group), (grouped, labels, lowest, highest, stored, stored_labels, owner_ids))
    maxsim = best.reshape(quads, DOCS // DOC_DEV, per_block).transpose(1, 2, 0).reshape(DOCS)
    return (embeddings, maxsim)
```

```python
import functools
import math

import jax
import jax.numpy as jnp
from jax import lax
from jax.experimental import pallas as pl
from jax.experimental.pallas import tpu as pltpu
from jax.sharding import PartitionSpec as P

MESH = pl.DeviceIdType.MESH
D = 768
HID = 3072
DOC = 64
MEM = 1024
CLUSTERS = 64
CHUNKS = 6
STEP = HID // CHUNKS
SCALE = 1.0 / math.sqrt(D)
LOWEST = -1e30 / SCALE
F32 = jnp.float32
BF16 = jnp.bfloat16


def iota(shape, dim):
    return lax.broadcasted_iota(jnp.int32, shape, dim)


def kernel(
    feat_h, dcl_h, gain_h, w1_h, bin_h, w2_h, mem_h, mcl_h, cr_h,
    emb_o, max_o,
    feat, dcl, gain, w1, bin_, w2, mem, mlab, cr,
    emb, sent, docs, memcol,
    lab_out, lab_z, lab_in, part, part_in, zmax, zin, row_out,
    load_sem, w_sem, out_sem,
    lz_s, lz_r, lp_s, lp_r, ml_s, ml_r, mm_s, mm_r,
    z_s, z_r, a_s, a_r, b_s, b_r, rp_s, rp_r, rz_s, rz_r,
):
    e = lax.axis_index("enc")
    o = lax.axis_index("own")
    x, c = e // 2, lax.rem(e, 2)
    z, y = o // 4, lax.rem(o, 4)
    a = x * (1 - c) + y * c
    b = y * (1 - c) + x * c

    def place(da, db, dz):
        pa, pb, pz = lax.rem(a + da, 4), lax.rem(b + db, 4), lax.rem(z + dz, 4)
        px = pa * (1 - c) + pb * c
        py = pb * (1 - c) + pa * c
        return (px * 2 + c, pz * 4 + py)

    other = (x * 2 + 1 - c, o)

    def remote(src, dst, ssem, rsem, where):
        return pltpu.make_async_remote_copy(
            src_ref=src, dst_ref=dst, send_sem=ssem, recv_sem=rsem,
            device_id=where, device_id_type=MESH,
        )

    def local(src, dst, sem):
        return pltpu.make_async_copy(src, dst, sem)

    small = [
        local(dcl_h, dcl, load_sem.at[0]),
        local(feat_h, feat, load_sem.at[1]),
        local(gain_h, gain, load_sem.at[2]),
        local(bin_h, bin_, load_sem.at[3]),
        local(cr_h, cr, load_sem.at[4]),
        local(mcl_h, mlab.at[0], load_sem.at[5]),
    ]
    for copy in small:
        copy.start()
    weights = []
    for j in range(CHUNKS):
        cols = pl.ds(j * STEP, STEP)
        weights.append((
            local(w1_h.at[:, cols], w1.at[:, cols], w_sem.at[0, j]),
            local(w2_h.at[cols], w2.at[cols], w_sem.at[1, j]),
        ))
        weights[-1][0].start()
        weights[-1][1].start()
    members = local(mem_h, mem.at[0], load_sem.at[6])

    plane = [(da, db) for db in range(4) for da in range(4) if (da, db) != (0, 0)]
    barrier = pltpu.get_barrier_semaphore()
    pl.semaphore_signal(barrier, inc=1, device_id=other, device_id_type=MESH)
    for d in (1, 2, 3):
        pl.semaphore_signal(barrier, inc=1, device_id=place(0, 0, d), device_id_type=MESH)
    for da, db in plane:
        pl.semaphore_signal(barrier, inc=1, device_id=place(da, db, 0), device_id_type=MESH)

    small[0].wait()
    k, lane = iota((DOC, 512), 0), iota((DOC, 512), 1)
    d, l = lane // 128, lane % 64
    hit = (k % 4 == (z + d) % 4) & (l // 16 == (4 - d) % 4) & (l % 16 == k // 4)
    spots = jnp.where(hit, 1.0, 0.0).astype(BF16)
    labels = jnp.broadcast_to(dcl[...].astype(F32), (8, DOC)).astype(BF16)
    spread = jnp.dot(labels, spots, preferred_element_type=F32)
    lab_z[0] = spread[:, :128]
    for d in (1, 2, 3):
        lab_out[d] = spread[:, d * 128 : (d + 1) * 128]

    pl.semaphore_wait(barrier, 4 + len(plane))
    lz = [remote(lab_out.at[d], lab_z.at[4 - d], lz_s.at[d], lz_r.at[4 - d], place(0, 0, d)) for d in (1, 2, 3)]
    for copy in lz:
        copy.start()
    small[5].wait()
    ml = remote(mlab.at[0], mlab.at[1], ml_s, ml_r, other)
    ml.start()

    small[1].wait()
    small[2].wait()
    r, k = iota((DOC, DOC), 0), iota((DOC, DOC), 1)
    order = jnp.where((k % 4 == (z + r // 16) % 4) & (k // 4 == r % 16), 1.0, 0.0).astype(BF16)
    inputs = jnp.dot(order, feat[...], preferred_element_type=F32)
    center = inputs - jnp.mean(inputs, axis=1, keepdims=True)
    spread = jnp.mean(center * center, axis=1, keepdims=True)
    normed = (center * lax.rsqrt(spread + 1e-05) * gain[...].reshape(1, D)).astype(BF16)
    small[3].wait()

    lp = [
        remote(lab_in.at[0, 0], lab_in.at[(4 - db) % 4, (4 - da) % 4],
               lp_s.at[db, da], lp_r.at[(4 - db) % 4, (4 - da) % 4], place(da, db, 0))
        for da, db in plane
    ]
    mm = remote(mem_h, mem.at[1], mm_s, mm_r, other)

    output = inputs
    for j in range(CHUNKS):
        weights[j][0].wait()
        pre = jnp.dot(normed, w1[:, j * STEP : (j + 1) * STEP], preferred_element_type=F32)
        hidden = jax.nn.gelu(pre + bin_[:, j * STEP : (j + 1) * STEP], approximate=True).astype(BF16)
        weights[j][1].wait()
        output = output + jnp.dot(hidden, w2[j * STEP : (j + 1) * STEP], preferred_element_type=F32)
        if j == 2:
            members.start()
            mm.start()
        if j == 3:
            for copy in lz:
                copy.wait_recv()
            lab_in[0, 0] = lab_z[0] + lab_z[1] + lab_z[2] + lab_z[3]
            for copy in lp:
                copy.start()
    found = (output * lax.rsqrt(jnp.mean(output * output, axis=1, keepdims=True) + 1e-06)).astype(BF16)
    sent[...] = found.reshape(4, 16, D)
    docs[0, 0, 0] = found[:16]

    zs = [remote(sent.at[d], docs.at[0, 0, 4 - d], z_s.at[d], z_r.at[4 - d], place(0, 0, d)) for d in (1, 2, 3)]
    for copy in zs:
        copy.start()

    k, r = iota((DOC, DOC), 0), iota((DOC, DOC), 1)
    back = jnp.where((k % 4 == (z + r // 16) % 4) & (k // 4 == r % 16), 1.0, 0.0).astype(BF16)
    emb[...] = jnp.dot(back, found, preferred_element_type=F32).astype(BF16)
    out = local(emb, emb_o, out_sem.at[0])
    out.start()

    A = {}
    B = {}

    def halves(dst, src, sem_s, sem_r, where, order):
        return {h: remote(src.at[pl.ds(2 * h, 2)], dst.at[pl.ds(2 * h, 2)], sem_s.at[h], sem_r.at[h], where) for h in order}

    A[3] = halves(docs.at[0, 3], docs.at[0, 0], a_s.at[3], a_r.at[3], place(1, 0, 0), (0, 1))
    A[1] = halves(docs.at[0, 1], docs.at[0, 0], a_s.at[1], a_r.at[1], place(3, 0, 0), (1, 0))
    A[2] = {
        0: remote(docs.at[0, 3, pl.ds(0, 2)], docs.at[0, 2, pl.ds(0, 2)], a_s.at[2, 0], a_r.at[2, 0], place(1, 0, 0)),
        1: remote(docs.at[0, 1, pl.ds(2, 2)], docs.at[0, 2, pl.ds(2, 2)], a_s.at[2, 1], a_r.at[2, 1], place(3, 0, 0)),
    }
    for da in range(4):
        B[da, 3] = halves(docs.at[3, da], docs.at[0, da], b_s.at[da, 3], b_r.at[da, 3], place(0, 1, 0), (0, 1))
        B[da, 1] = halves(docs.at[1, da], docs.at[0, da], b_s.at[da, 1], b_r.at[da, 1], place(0, 3, 0), (1, 0))
        B[da, 2] = {
            0: remote(docs.at[3, da, pl.ds(0, 2)], docs.at[2, da, pl.ds(0, 2)], b_s.at[da, 2, 0], b_r.at[da, 2, 0], place(0, 1, 0)),
            1: remote(docs.at[1, da, pl.ds(2, 2)], docs.at[2, da, pl.ds(2, 2)], b_s.at[da, 2, 1], b_r.at[da, 2, 1], place(0, 3, 0)),
        }

    for copy in zs:
        copy.wait_recv()
    A[3][0].start()
    A[1][1].start()
    A[3][1].start()
    A[1][0].start()

    def send_b(da):
        B[da, 3][0].start()
        B[da, 1][1].start()
        B[da, 3][1].start()
        B[da, 1][0].start()

    send_b(0)

    small[4].wait()
    ml.wait_recv()
    number = iota((1, CLUSTERS), 1)
    inside = (cr[0:1] <= o) & (o <= cr[1:2])
    named = jnp.where(inside, number, -1).astype(F32)
    square = iota((CLUSTERS, CLUSTERS), 0) == iota((CLUSTERS, CLUSTERS), 1)
    table = jnp.dot(
        jnp.where(square, named, 0.0).astype(BF16), jnp.ones((CLUSTERS, 128), BF16), preferred_element_type=F32
    ).astype(BF16)
    eye = iota((128, 128), 0) == iota((128, 128), 1)
    ones = jnp.ones((128, 128), BF16)
    for half in range(2):
        for i in range(8):
            row = mlab[half, i : i + 1, :].astype(F32)
            col = jnp.dot(jnp.where(eye, row, 0.0).astype(BF16), ones, preferred_element_type=F32)
            onehot = jnp.where(col[:, :CLUSTERS] == iota((128, CLUSTERS), 1).astype(F32), 1.0, 0.0).astype(BF16)
            memcol[pl.ds((half * 8 + i) * 128, 128), :] = jnp.dot(onehot, table, preferred_element_type=F32)
    for copy in lp:
        copy.wait_recv()

    A[3][0].wait_recv()
    A[2][0].start()
    A[1][1].wait_recv()
    A[2][1].start()
    A[3][1].wait_recv()
    A[1][0].wait_recv()
    send_b(3)
    send_b(1)
    A[2][0].wait_recv()
    A[2][1].wait_recv()
    send_b(2)

    def pass_on(da):
        B[da, 3][0].wait_recv()
        B[da, 2][0].start()
        B[da, 1][1].wait_recv()
        B[da, 2][1].start()

    low = iota((8, 128), 1) < 64
    copies = {}

    def match(db):
        block = docs[db].reshape(256, D)
        rows = [jnp.where(low, lab_in[db, 2 * h], lab_in[db, 2 * h + 1])[:1] for h in range(2)]
        best = [jnp.full((8, 128), LOWEST, F32)] * 2
        for i in range(4):
            stock = mem[i // 2, pl.ds((i % 2) * 512, 512), :]
            score = lax.dot_general(stock, block, (((1,), (1,)), ((), ())), preferred_element_type=F32)
            column = memcol[pl.ds(i * 512, 512), :]
            for h in range(2):
                kept = jnp.where(column == rows[h], score[:, h * 128 : (h + 1) * 128], LOWEST)
                best[h] = jnp.maximum(best[h], jnp.max(kept.reshape(64, 8, 128), axis=0))
        for h in range(2):
            part[db, h] = best[h]
        for da in range(4):
            if (da, db) == (0, 0):
                continue
            s, t = (4 - db) % 4, (4 - da) % 4
            copies[da, db] = remote(part.at[db, da // 2], part_in.at[s, t], rp_s.at[db, da], rp_r.at[s, t], place(da, db, 0))
            copies[da, db].start()

    pass_on(0)
    members.wait()
    mm.wait_recv()
    match(0)
    pass_on(3)
    pass_on(1)
    pass_on(2)
    for da in range(4):
        B[da, 3][1].wait_recv()
    match(3)
    for da in range(4):
        B[da, 1][0].wait_recv()
    match(1)
    for da in range(4):
        B[da, 2][0].wait_recv()
        B[da, 2][1].wait_recv()
    match(2)

    best = [part[0, 0], jnp.full((8, 128), LOWEST, F32)]
    for da, db in plane:
        s, t = (4 - db) % 4, (4 - da) % 4
        copies[da, db].wait_recv()
    for da, db in plane:
        s, t = (4 - db) % 4, (4 - da) % 4
        best[da % 2] = jnp.maximum(best[da % 2], part_in[s, t])
    merged = jnp.maximum(best[0], pltpu.roll(best[1], 64, axis=1))
    zmax[...] = merged
    rz = [remote(zmax, zin.at[4 - d], rz_s.at[d], rz_r.at[4 - d], place(0, 0, d)) for d in (1, 2, 3)]
    for copy in rz:
        copy.start()
    lane = iota((8, 128), 1)
    final = merged
    for copy in rz:
        copy.wait_recv()
    for d in (1, 2, 3):
        final = jnp.where(lane // 16 == d, zin[4 - d], final)
    final = jnp.max(final, axis=0, keepdims=True)[:, :DOC]
    l, k = iota((DOC, DOC), 0), iota((DOC, DOC), 1)
    column = jnp.max(jnp.where(l == k, final, LOWEST), axis=1, keepdims=True)
    takes = (k // 4 == l % 16) & (k % 4 == (z - l // 16 + 4) % 4)
    row = jnp.max(jnp.where(takes, column, LOWEST), axis=0, keepdims=True) * SCALE
    row_out[...] = row
    last = local(row_out, max_o, out_sem.at[1])
    last.start()
    last.wait()
    out.wait()

    for copy in (*lz, *lp, ml, mm, *zs, *copies.values(), *rz):
        copy.wait_send()
    for group in (*A.values(), *B.values()):
        for copy in group.values():
            copy.wait_send()


def step(features, doc_cluster, norm_gain, w_in, b_in, w_out, members, member_cluster, cluster_range):
    dma = pltpu.SemaphoreType.DMA
    anywhere = pl.BlockSpec(memory_space=pltpu.HBM)
    embeddings, best = pl.pallas_call(
        kernel,
        out_shape=(jax.ShapeDtypeStruct((DOC, D), BF16), jax.ShapeDtypeStruct((1, DOC), F32)),
        in_specs=[anywhere] * 9,
        out_specs=(anywhere, anywhere),
        scratch_shapes=[
            pltpu.VMEM((DOC, D), BF16),
            pltpu.VMEM((1, DOC), jnp.int32),
            pltpu.VMEM((D,), F32),
            pltpu.VMEM((D, HID), BF16),
            pltpu.VMEM((1, HID), F32),
            pltpu.VMEM((HID, D), BF16),
            pltpu.VMEM((2, MEM, D), BF16),
            pltpu.VMEM((2, 8, 128), jnp.int32),
            pltpu.VMEM((2, CLUSTERS), jnp.int32),
            pltpu.VMEM((DOC, D), BF16),
            pltpu.VMEM((4, 16, D), BF16),
            pltpu.VMEM((4, 4, 4, 16, D), BF16),
            pltpu.VMEM((2 * MEM, 128), F32),
            pltpu.VMEM((4, 8, 128), F32),
            pltpu.VMEM((4, 8, 128), F32),
            pltpu.VMEM((4, 4, 8, 128), F32),
            pltpu.VMEM((4, 2, 8, 128), F32),
            pltpu.VMEM((4, 4, 8, 128), F32),
            pltpu.VMEM((8, 128), F32),
            pltpu.VMEM((4, 8, 128), F32),
            pltpu.VMEM((1, DOC), F32),
            dma((7,)), dma((2, CHUNKS)), dma((2,)),
            dma((4,)), dma((4,)), dma((4, 4)), dma((4, 4)), dma, dma, dma, dma,
            dma((4,)), dma((4,)), dma((4, 2)), dma((4, 2)), dma((4, 4, 2)), dma((4, 4, 2)),
            dma((4, 4)), dma((4, 4)), dma((4,)), dma((4,)),
        ],
        compiler_params=pltpu.CompilerParams(
            collective_id=0, has_side_effects=True, vmem_limit_bytes=64 * 2**20
        ),
    )(
        features, doc_cluster.reshape(1, DOC), norm_gain, w_in, b_in.reshape(1, HID), w_out,
        members.reshape(MEM, D), member_cluster.reshape(8, 128), cluster_range.T,
    )
    return embeddings, best.reshape(DOC)


def solution(mesh):
    placed = (
        P(("enc", "own"), None), P(("enc", "own")), P(), P(), P(), P(),
        P("own", "enc", None), P("own", "enc"), P(),
    )
    return jax.shard_map(
        step, mesh=mesh, in_specs=placed, out_specs=(P(("enc", "own"), None), P(("enc", "own"))), check_vma=False
    )
```

```python
import functools
import math

import jax
import jax.numpy as jnp
from jax import lax
from jax.experimental import pallas as pl
from jax.experimental.pallas import tpu as pltpu
from jax.sharding import PartitionSpec as P

MESH = pl.DeviceIdType.MESH
D = 768
HID = 3072
DOC = 64
MEM = 1024
CLUSTERS = 64
CHUNKS = 6
WINDOW = 3
STEP = HID // CHUNKS
SCALE = 1.0 / math.sqrt(D)
LOWEST = -1e30 / SCALE
F32 = jnp.float32
BF16 = jnp.bfloat16


def iota(shape, dim):
    return lax.broadcasted_iota(jnp.int32, shape, dim)


def kernel(
    feat_h, dcl_h, gain_h, w1_h, bin_h, w2_h, mem_h, mcl_h, cr_h,
    emb_o, max_o,
    feat, dcl, gain, w1, bin_, w2, mem, mlab, cr,
    sent, docs, memcol,
    lab_out, lab_z, lab_in, part, part_in, most, most_in,
    load_sem, w_sem,
    lz_s, lz_r, lp_s, lp_r, ml_s, ml_r, mm_s, mm_r,
    z_s, z_r, b_s, b_r, rp_s, rp_r, rz_s, rz_r,
):
    e = lax.axis_index("enc")
    o = lax.axis_index("own")
    x, c = e // 2, lax.rem(e, 2)
    z, y = o // 4, lax.rem(o, 4)
    a = x * (1 - c) + y * c
    b = y * (1 - c) + x * c

    def place(da, db, dz):
        pa, pb, pz = lax.rem(a + da, 4), lax.rem(b + db, 4), lax.rem(z + dz, 4)
        px = pa * (1 - c) + pb * c
        py = pb * (1 - c) + pa * c
        return (px * 2 + c, pz * 4 + py)

    other = (x * 2 + 1 - c, o)

    def remote(src, dst, ssem, rsem, where):
        return pltpu.make_async_remote_copy(
            src_ref=src, dst_ref=dst, send_sem=ssem, recv_sem=rsem,
            device_id=where, device_id_type=MESH,
        )

    def local(src, dst, sem):
        return pltpu.make_async_copy(src, dst, sem)

    small = [
        local(dcl_h, dcl, load_sem.at[0]),
        local(feat_h, feat, load_sem.at[1]),
        local(gain_h, gain, load_sem.at[2]),
        local(bin_h, bin_, load_sem.at[3]),
        local(cr_h, cr, load_sem.at[4]),
        local(mcl_h, mlab.at[0], load_sem.at[5]),
    ]
    for copy in small:
        copy.start()
    weights = []
    for j in range(CHUNKS):
        cols = pl.ds(j * STEP, STEP)
        weights.append((
            local(w1_h.at[:, cols], w1.at[:, cols], w_sem.at[0, j]),
            local(w2_h.at[cols], w2.at[cols], w_sem.at[1, j]),
        ))
        if j < WINDOW:
            weights[-1][0].start()
            weights[-1][1].start()
    members = local(mem_h, mem.at[0], load_sem.at[6])

    near = [(da, dz) for da in (0, 2, 1, 3) for dz in (2, 1, 3, 0) if (da, dz) != (0, 0)]
    barrier = pltpu.get_barrier_semaphore()
    pl.semaphore_signal(barrier, inc=1, device_id=other, device_id_type=MESH)
    for db in (1, 2, 3):
        pl.semaphore_signal(barrier, inc=1, device_id=place(0, db, 0), device_id_type=MESH)
    for da, dz in near:
        pl.semaphore_signal(barrier, inc=1, device_id=place(da, 0, dz), device_id_type=MESH)

    small[0].wait()
    k, lane = iota((DOC, 512), 0), iota((DOC, 512), 1)
    d, l = lane // 128, lane % 64
    hit = (k % 4 == (z + d) % 4) & (l // 16 == (4 - d) % 4) & (l % 16 == k // 4)
    spots = jnp.where(hit, 1.0, 0.0).astype(BF16)
    labels = jnp.broadcast_to(dcl[...].astype(F32), (8, DOC)).astype(BF16)
    spread = jnp.dot(labels, spots, preferred_element_type=F32)
    lab_z[0, 0] = spread[:, :128]
    for d in range(4):
        lab_out[d] = spread[:, d * 128 : (d + 1) * 128]

    pl.semaphore_wait(barrier, 4 + len(near))
    lz = [
        remote(lab_out.at[dz], lab_z.at[-da % 4, -dz % 4], lz_s.at[da, dz], lz_r.at[-da % 4, -dz % 4], place(da, 0, dz))
        for da, dz in near
    ]
    for copy in lz:
        copy.start()
    small[5].wait()
    ml = remote(mlab.at[0], mlab.at[1], ml_s, ml_r, other)
    ml.start()

    small[1].wait()
    small[2].wait()
    r, k = iota((DOC, DOC), 0), iota((DOC, DOC), 1)
    order = jnp.where((k % 4 == (z + r // 16) % 4) & (k // 4 == r % 16), 1.0, 0.0).astype(BF16)
    inputs = jnp.dot(order, feat[...], preferred_element_type=F32)
    center = inputs - jnp.mean(inputs, axis=1, keepdims=True)
    spread = jnp.mean(center * center, axis=1, keepdims=True)
    normed = (center * lax.rsqrt(spread + 1e-05) * gain[...].reshape(1, D)).astype(BF16)
    small[3].wait()

    low = iota((8, 128), 1) < 64
    lp = [remote(lab_in.at[0], lab_in.at[4 - db], lp_s.at[db], lp_r.at[4 - db], place(0, db, 0)) for db in (1, 2, 3)]
    mm = remote(mem_h, mem.at[1], mm_s, mm_r, other)

    output = inputs
    for j in range(CHUNKS):
        weights[j][0].wait()
        pre = jnp.dot(normed, w1[:, j * STEP : (j + 1) * STEP], preferred_element_type=F32)
        hidden = jax.nn.gelu(pre + bin_[:, j * STEP : (j + 1) * STEP], approximate=True).astype(BF16)
        weights[j][1].wait()
        output = output + jnp.dot(hidden, w2[j * STEP : (j + 1) * STEP], preferred_element_type=F32)
        if j + WINDOW < CHUNKS:
            weights[j + WINDOW][0].start()
            weights[j + WINDOW][1].start()
        if j == 3:
            members.start()
            mm.start()
        if j == 5:
            for copy in lz:
                copy.wait_recv()
            sums = [lab_z[da, 0] + lab_z[da, 1] + lab_z[da, 2] + lab_z[da, 3] for da in range(4)]
            lab_in[0, 0] = jnp.where(low, sums[0], sums[1])
            lab_in[0, 1] = jnp.where(low, sums[2], sums[3])
            for copy in lp:
                copy.start()
    found = (output * lax.rsqrt(jnp.mean(output * output, axis=1, keepdims=True) + 1e-06)).astype(BF16)
    sent[...] = found.reshape(4, 16, D)
    docs[0, 0, 0] = found[:16]

    zs = {
        (-da % 4, -dz % 4): remote(
            sent.at[dz], docs.at[0, -da % 4, -dz % 4], z_s.at[da, dz], z_r.at[-da % 4, -dz % 4], place(da, 0, dz)
        )
        for da, dz in near
    }
    for copy in zs.values():
        copy.start()

    k, r = iota((DOC, DOC), 0), iota((DOC, DOC), 1)
    back = jnp.where((k % 4 == (z + r // 16) % 4) & (k // 4 == r % 16), 1.0, 0.0).astype(BF16)
    emb_o[...] = jnp.dot(back, found, preferred_element_type=F32).astype(BF16)

    B = {}

    def halves(dst, src, sem_s, sem_r, where, order):
        return {h: remote(src.at[pl.ds(2 * h, 2)], dst.at[pl.ds(2 * h, 2)], sem_s.at[h], sem_r.at[h], where) for h in order}

    for da in range(4):
        B[da, 3] = halves(docs.at[3, da], docs.at[0, da], b_s.at[da, 3], b_r.at[da, 3], place(0, 1, 0), (0, 1))
        B[da, 1] = halves(docs.at[1, da], docs.at[0, da], b_s.at[da, 1], b_r.at[da, 1], place(0, 3, 0), (1, 0))
        B[da, 2] = {
            0: remote(docs.at[3, da, pl.ds(0, 2)], docs.at[2, da, pl.ds(0, 2)], b_s.at[da, 2, 0], b_r.at[da, 2, 0], place(0, 1, 0)),
            1: remote(docs.at[1, da, pl.ds(2, 2)], docs.at[2, da, pl.ds(2, 2)], b_s.at[da, 2, 1], b_r.at[da, 2, 1], place(0, 3, 0)),
        }

    def send_b(da):
        for dz in range(4):
            if (da, dz) in zs:
                zs[da, dz].wait_recv()
        B[da, 3][0].start()
        B[da, 1][1].start()
        B[da, 3][1].start()
        B[da, 1][0].start()

    small[4].wait()
    ml.wait_recv()
    number = iota((1, CLUSTERS), 1)
    inside = (cr[0:1] <= o) & (o <= cr[1:2])
    named = jnp.where(inside, number, -1).astype(F32)
    square = iota((CLUSTERS, CLUSTERS), 0) == iota((CLUSTERS, CLUSTERS), 1)
    table = jnp.dot(
        jnp.where(square, named, 0.0).astype(BF16), jnp.ones((CLUSTERS, 128), BF16), preferred_element_type=F32
    ).astype(BF16)
    eye = iota((128, 128), 0) == iota((128, 128), 1)
    ones = jnp.ones((128, 128), BF16)
    for half in range(2):
        for i in range(8):
            row = mlab[half, i : i + 1, :].astype(F32)
            col = jnp.dot(jnp.where(eye, row, 0.0).astype(BF16), ones, preferred_element_type=F32)
            onehot = jnp.where(col[:, :CLUSTERS] == iota((128, CLUSTERS), 1).astype(F32), 1.0, 0.0).astype(BF16)
            memcol[pl.ds((half * 8 + i) * 128, 128), :] = jnp.dot(onehot, table, preferred_element_type=F32)
    for da in (0, 2, 1, 3):
        send_b(da)
    for copy in lp:
        copy.wait_recv()

    def pass_on(da):
        B[da, 3][0].wait_recv()
        B[da, 2][0].start()
        B[da, 1][1].wait_recv()
        B[da, 2][1].start()

    copies = []

    def match(db):
        block = docs[db].reshape(256, D)
        rows = [lab_in[db, h, :1] for h in range(2)]
        best = [jnp.full((8, 128), LOWEST, F32)] * 2
        for i in range(4):
            stock = mem[i // 2, pl.ds((i % 2) * 512, 512), :]
            score = lax.dot_general(stock, block, (((1,), (1,)), ((), ())), preferred_element_type=F32)
            column = memcol[pl.ds(i * 512, 512), :]
            for h in range(2):
                kept = jnp.where(column == rows[h], score[:, h * 128 : (h + 1) * 128], LOWEST)
                best[h] = jnp.maximum(best[h], jnp.max(kept.reshape(64, 8, 128), axis=0))
        for h in range(2):
            part[db, h] = best[h]
        if db:
            copies.append(remote(part.at[db], part_in.at[-db % 4], rp_s.at[db], rp_r.at[-db % 4], place(0, db, 0)))
            copies[-1].start()

    pass_on(0)
    members.wait()
    mm.wait_recv()
    match(0)
    for da in (2, 1, 3):
        pass_on(da)
    for da in range(4):
        B[da, 3][1].wait_recv()
    match(3)
    for da in range(4):
        B[da, 1][0].wait_recv()
    match(1)
    for da in range(4):
        B[da, 2][0].wait_recv()
        B[da, 2][1].wait_recv()
    match(2)

    for copy in copies:
        copy.wait_recv()
    most[...] = jnp.maximum(jnp.maximum(part[0], part_in[1]), jnp.maximum(part_in[2], part_in[3]))
    rz = [
        remote(most.at[da // 2], most_in.at[-da % 4, -dz % 4], rz_s.at[da, dz], rz_r.at[-da % 4, -dz % 4], place(da, 0, dz))
        for da, dz in near
    ]
    for copy in rz:
        copy.start()
    for copy in (*lz, *lp, ml, mm, *zs.values(), *copies):
        copy.wait_send()
    for group in B.values():
        for copy in group.values():
            copy.wait_send()
    most_in[0, 0] = most[0]
    for copy in rz:
        copy.wait_recv()
    quarter = iota((8, 128), 1) % 64 // 16
    sides = []
    for odd in range(2):
        side = jnp.full((8, 128), LOWEST, F32)
        for s in range(4):
            side = jnp.where(quarter == -s % 4, jnp.maximum(most_in[odd, s], most_in[odd + 2, s]), side)
        sides.append(side)
    final = jnp.maximum(sides[0], pltpu.roll(sides[1], 64, axis=1))
    final = jnp.max(final, axis=0, keepdims=True)[:, :DOC]
    l, k = iota((DOC, DOC), 0), iota((DOC, DOC), 1)
    column = jnp.max(jnp.where(l == k, final, LOWEST), axis=1, keepdims=True)
    takes = (k // 4 == l % 16) & (k % 4 == (z - l // 16 + 4) % 4)
    max_o[...] = jnp.max(jnp.where(takes, column, LOWEST), axis=0, keepdims=True) * SCALE
    for copy in rz:
        copy.wait_send()


def hand_on(embeddings, best, emb_o, max_o):
    emb_o[...] = embeddings[...]
    max_o[...] = best[...]


def step(features, doc_cluster, norm_gain, w_in, b_in, w_out, members, member_cluster, cluster_range):
    dma = pltpu.SemaphoreType.DMA
    anywhere = pl.BlockSpec(memory_space=pltpu.HBM)
    embeddings, best = pl.pallas_call(
        kernel,
        out_shape=(jax.ShapeDtypeStruct((DOC, D), BF16), jax.ShapeDtypeStruct((1, DOC), F32)),
        in_specs=[anywhere] * 9,
        out_specs=(pl.BlockSpec(memory_space=pltpu.VMEM), pl.BlockSpec(memory_space=pltpu.VMEM)),
        scratch_shapes=[
            pltpu.VMEM((DOC, D), BF16),
            pltpu.VMEM((1, DOC), jnp.int32),
            pltpu.VMEM((D,), F32),
            pltpu.VMEM((D, HID), BF16),
            pltpu.VMEM((1, HID), F32),
            pltpu.VMEM((HID, D), BF16),
            pltpu.VMEM((2, MEM, D), BF16),
            pltpu.VMEM((2, 8, 128), jnp.int32),
            pltpu.VMEM((2, CLUSTERS), jnp.int32),
            pltpu.VMEM((4, 16, D), BF16),
            pltpu.VMEM((4, 4, 4, 16, D), BF16),
            pltpu.VMEM((2 * MEM, 128), F32),
            pltpu.VMEM((4, 8, 128), F32),
            pltpu.VMEM((4, 4, 8, 128), F32),
            pltpu.VMEM((4, 2, 8, 128), F32),
            pltpu.VMEM((4, 2, 8, 128), F32),
            pltpu.VMEM((4, 2, 8, 128), F32),
            pltpu.VMEM((2, 8, 128), F32),
            pltpu.VMEM((4, 4, 8, 128), F32),
            dma((7,)), dma((2, CHUNKS)),
            dma((4, 4)), dma((4, 4)), dma((4,)), dma((4,)), dma, dma, dma, dma,
            dma((4, 4)), dma((4, 4)), dma((4, 4, 2)), dma((4, 4, 2)),
            dma((4,)), dma((4,)), dma((4, 4)), dma((4, 4)),
        ],
        compiler_params=pltpu.CompilerParams(
            collective_id=0, has_side_effects=True, vmem_limit_bytes=64 * 2**20
        ),
    )(
        features, doc_cluster.reshape(1, DOC), norm_gain, w_in, b_in.reshape(1, HID), w_out,
        members.reshape(MEM, D), member_cluster.reshape(8, 128), cluster_range.T,
    )
    embeddings, best = pl.pallas_call(
        hand_on,
        out_shape=(jax.ShapeDtypeStruct((DOC, D), BF16), jax.ShapeDtypeStruct((1, DOC), F32)),
        in_specs=[pl.BlockSpec(memory_space=pltpu.VMEM)] * 2,
        out_specs=(pl.BlockSpec(memory_space=pltpu.VMEM), pl.BlockSpec(memory_space=pltpu.VMEM)),
    )(embeddings, best)
    return embeddings, best.reshape(DOC)


def solution(mesh):
    placed = (
        P(("enc", "own"), None), P(("enc", "own")), P(), P(), P(), P(),
        P("own", "enc", None), P("own", "enc"), P(),
    )
    return jax.shard_map(
        step, mesh=mesh, in_specs=placed, out_specs=(P(("enc", "own"), None), P(("enc", "own"))), check_vma=False
    )
```

```python
import functools
import math

import jax
import jax.numpy as jnp
from jax import lax
from jax.experimental import pallas as pl
from jax.experimental.pallas import tpu as pltpu
from jax.sharding import PartitionSpec as P

MESH = pl.DeviceIdType.MESH
D = 768
HID = 3072
DOC = 64
MEM = 1024
CLUSTERS = 64
CHUNKS = 6
WINDOW = 3
STEP = HID // CHUNKS
SCALE = 1.0 / math.sqrt(D)
LOWEST = -1e30 / SCALE
F32 = jnp.float32
BF16 = jnp.bfloat16


def iota(shape, dim):
    return lax.broadcasted_iota(jnp.int32, shape, dim)


def kernel(
    feat_h, dcl_h, gain_h, w1_h, bin_h, w2_h, mem_h, mcl_h, cr_h,
    emb_o, max_o,
    feat, dcl, gain, w1, bin_, w2, mem, mlab, cr,
    sent, docs, memcol,
    lab_out, lab_z, lab_in, part, part_in, most, most_in,
    load_sem, w_sem,
    lz_s, lz_r, lp_s, lp_r, ml_s, ml_r, mm_s, mm_r,
    z_s, z_r, b_s, b_r, rp_s, rp_r, rz_s, rz_r,
):
    e = lax.axis_index("enc")
    o = lax.axis_index("own")
    x, c = e // 2, lax.rem(e, 2)
    z, y = o // 4, lax.rem(o, 4)
    a = x * (1 - c) + y * c
    b = y * (1 - c) + x * c

    def place(da, db, dz):
        pa, pb, pz = lax.rem(a + da, 4), lax.rem(b + db, 4), lax.rem(z + dz, 4)
        px = pa * (1 - c) + pb * c
        py = pb * (1 - c) + pa * c
        return (px * 2 + c, pz * 4 + py)

    other = (x * 2 + 1 - c, o)

    def remote(src, dst, ssem, rsem, where):
        return pltpu.make_async_remote_copy(
            src_ref=src, dst_ref=dst, send_sem=ssem, recv_sem=rsem,
            device_id=where, device_id_type=MESH,
        )

    def local(src, dst, sem):
        return pltpu.make_async_copy(src, dst, sem)

    small = [
        local(dcl_h, dcl, load_sem.at[0]),
        local(feat_h, feat, load_sem.at[1]),
        local(gain_h, gain, load_sem.at[2]),
        local(bin_h, bin_, load_sem.at[3]),
        local(cr_h, cr, load_sem.at[4]),
        local(mcl_h, mlab.at[0], load_sem.at[5]),
    ]
    for copy in small:
        copy.start()
    weights = []
    for j in range(CHUNKS):
        cols = pl.ds(j * STEP, STEP)
        weights.append((
            local(w1_h.at[:, cols], w1.at[:, cols], w_sem.at[0, j]),
            local(w2_h.at[cols], w2.at[cols], w_sem.at[1, j]),
        ))
        if j < WINDOW:
            weights[-1][0].start()
            weights[-1][1].start()
    members = local(mem_h, mem.at[0], load_sem.at[6])

    near = [(da, dz) for da in (0, 2, 1, 3) for dz in (2, 1, 3, 0) if (da, dz) != (0, 0)]
    barrier = pltpu.get_barrier_semaphore()
    pl.semaphore_signal(barrier, inc=1, device_id=other, device_id_type=MESH)
    for db in (1, 2, 3):
        pl.semaphore_signal(barrier, inc=1, device_id=place(0, db, 0), device_id_type=MESH)
    for da, dz in near:
        pl.semaphore_signal(barrier, inc=1, device_id=place(da, 0, dz), device_id_type=MESH)

    small[0].wait()
    k, lane = iota((DOC, 512), 0), iota((DOC, 512), 1)
    d, l = lane // 128, lane % 64
    hit = (k % 4 == (z + d) % 4) & (l // 16 == (4 - d) % 4) & (l % 16 == k // 4)
    spots = jnp.where(hit, 1.0, 0.0).astype(BF16)
    labels = jnp.broadcast_to(dcl[...].astype(F32), (8, DOC)).astype(BF16)
    spread = jnp.dot(labels, spots, preferred_element_type=F32)
    lab_z[0, 0] = spread[:, :128]
    for d in range(4):
        lab_out[d] = spread[:, d * 128 : (d + 1) * 128]

    lz = [
        remote(lab_out.at[dz], lab_z.at[-da % 4, -dz % 4], lz_s.at[da, dz], lz_r.at[-da % 4, -dz % 4], place(da, 0, dz))
        for da, dz in near
    ]
    small[5].wait()
    ml = remote(mlab.at[0], mlab.at[1], ml_s, ml_r, other)

    small[1].wait()
    small[2].wait()
    r, k = iota((DOC, DOC), 0), iota((DOC, DOC), 1)
    order = jnp.where((k % 4 == (z + r // 16) % 4) & (k // 4 == r % 16), 1.0, 0.0).astype(BF16)
    inputs = jnp.dot(order, feat[...], preferred_element_type=F32)
    center = inputs - jnp.mean(inputs, axis=1, keepdims=True)
    spread = jnp.mean(center * center, axis=1, keepdims=True)
    normed = (center * lax.rsqrt(spread + 1e-05) * gain[...].reshape(1, D)).astype(BF16)
    small[3].wait()

    low = iota((8, 128), 1) < 64
    lp = [remote(lab_in.at[0], lab_in.at[4 - db], lp_s.at[db], lp_r.at[4 - db], place(0, db, 0)) for db in (1, 2, 3)]
    mm = remote(mem_h, mem.at[1], mm_s, mm_r, other)

    output = inputs
    for j in range(CHUNKS):
        weights[j][0].wait()
        pre = jnp.dot(normed, w1[:, j * STEP : (j + 1) * STEP], preferred_element_type=F32)
        hidden = jax.nn.gelu(pre + bin_[:, j * STEP : (j + 1) * STEP], approximate=True).astype(BF16)
        weights[j][1].wait()
        output = output + jnp.dot(hidden, w2[j * STEP : (j + 1) * STEP], preferred_element_type=F32)
        if j + WINDOW < CHUNKS:
            weights[j + WINDOW][0].start()
            weights[j + WINDOW][1].start()
        if j == 2:
            pl.semaphore_wait(barrier, 4 + len(near))
            for copy in lz:
                copy.start()
            ml.start()
        if j == 3:
            members.start()
            mm.start()
    found = (output * lax.rsqrt(jnp.mean(output * output, axis=1, keepdims=True) + 1e-06)).astype(BF16)
    sent[...] = found.reshape(4, 16, D)
    docs[0, 0, 0] = found[:16]

    zs = {
        (-da % 4, -dz % 4): remote(
            sent.at[dz], docs.at[0, -da % 4, -dz % 4], z_s.at[da, dz], z_r.at[-da % 4, -dz % 4], place(da, 0, dz)
        )
        for da, dz in near
    }
    for copy in zs.values():
        copy.start()

    k, r = iota((DOC, DOC), 0), iota((DOC, DOC), 1)
    back = jnp.where((k % 4 == (z + r // 16) % 4) & (k // 4 == r % 16), 1.0, 0.0).astype(BF16)
    emb_o[...] = jnp.dot(back, found, preferred_element_type=F32).astype(BF16)

    B = {}

    def halves(dst, src, sem_s, sem_r, where, order):
        return {h: remote(src.at[pl.ds(2 * h, 2)], dst.at[pl.ds(2 * h, 2)], sem_s.at[h], sem_r.at[h], where) for h in order}

    for da in range(4):
        B[da, 3] = halves(docs.at[3, da], docs.at[0, da], b_s.at[da, 3], b_r.at[da, 3], place(0, 1, 0), (0, 1))
        B[da, 1] = halves(docs.at[1, da], docs.at[0, da], b_s.at[da, 1], b_r.at[da, 1], place(0, 3, 0), (1, 0))
        B[da, 2] = {
            0: remote(docs.at[3, da, pl.ds(0, 2)], docs.at[2, da, pl.ds(0, 2)], b_s.at[da, 2, 0], b_r.at[da, 2, 0], place(0, 1, 0)),
            1: remote(docs.at[1, da, pl.ds(2, 2)], docs.at[2, da, pl.ds(2, 2)], b_s.at[da, 2, 1], b_r.at[da, 2, 1], place(0, 3, 0)),
        }

    def send_b(da):
        for dz in range(4):
            if (da, dz) in zs:
                zs[da, dz].wait_recv()
        B[da, 3][0].start()
        B[da, 1][1].start()

    def send_rest(da):
        B[da, 3][1].start()
        B[da, 1][0].start()

    for copy in lz:
        copy.wait_recv()
    sums = [lab_z[da, 0] + lab_z[da, 1] + lab_z[da, 2] + lab_z[da, 3] for da in range(4)]
    lab_in[0, 0] = jnp.where(low, sums[0], sums[1])
    lab_in[0, 1] = jnp.where(low, sums[2], sums[3])
    for copy in lp:
        copy.start()

    small[4].wait()
    ml.wait_recv()
    number = iota((1, CLUSTERS), 1)
    inside = (cr[0:1] <= o) & (o <= cr[1:2])
    named = jnp.where(inside, number, -1).astype(F32)
    square = iota((CLUSTERS, CLUSTERS), 0) == iota((CLUSTERS, CLUSTERS), 1)
    table = jnp.dot(
        jnp.where(square, named, 0.0).astype(BF16), jnp.ones((CLUSTERS, 128), BF16), preferred_element_type=F32
    ).astype(BF16)
    eye = iota((128, 128), 0) == iota((128, 128), 1)
    ones = jnp.ones((128, 128), BF16)
    for half in range(2):
        for i in range(8):
            row = mlab[half, i : i + 1, :].astype(F32)
            col = jnp.dot(jnp.where(eye, row, 0.0).astype(BF16), ones, preferred_element_type=F32)
            onehot = jnp.where(col[:, :CLUSTERS] == iota((128, CLUSTERS), 1).astype(F32), 1.0, 0.0).astype(BF16)
            memcol[pl.ds((half * 8 + i) * 128, 128), :] = jnp.dot(onehot, table, preferred_element_type=F32)
    def pass_on(da):
        B[da, 3][0].wait_recv()
        B[da, 2][0].start()
        B[da, 1][1].wait_recv()
        B[da, 2][1].start()

    send_b(0)
    send_b(2)
    send_b(1)
    send_b(3)
    send_rest(0)
    send_rest(2)
    send_rest(1)
    send_rest(3)
    pass_on(0)
    pass_on(2)
    pass_on(1)
    pass_on(3)
    for copy in lp:
        copy.wait_recv()

    copies = []

    def match(db):
        block = docs[db].reshape(256, D)
        rows = [lab_in[db, h, :1] for h in range(2)]
        best = [jnp.full((8, 128), LOWEST, F32)] * 2
        for i in range(4):
            stock = mem[i // 2, pl.ds((i % 2) * 512, 512), :]
            score = lax.dot_general(stock, block, (((1,), (1,)), ((), ())), preferred_element_type=F32)
            column = memcol[pl.ds(i * 512, 512), :]
            for h in range(2):
                kept = jnp.where(column == rows[h], score[:, h * 128 : (h + 1) * 128], LOWEST)
                best[h] = jnp.maximum(best[h], jnp.max(kept.reshape(64, 8, 128), axis=0))
        for h in range(2):
            part[db, h] = best[h]
        if db:
            copies.append(remote(part.at[db], part_in.at[-db % 4], rp_s.at[db], rp_r.at[-db % 4], place(0, db, 0)))
            copies[-1].start()

    members.wait()
    mm.wait_recv()
    match(0)
    for da in range(4):
        B[da, 3][1].wait_recv()
    match(3)
    for da in range(4):
        B[da, 1][0].wait_recv()
    match(1)
    for da in range(4):
        B[da, 2][0].wait_recv()
        B[da, 2][1].wait_recv()
    match(2)

    for copy in copies:
        copy.wait_recv()
    most[...] = jnp.maximum(jnp.maximum(part[0], part_in[1]), jnp.maximum(part_in[2], part_in[3]))
    rz = [
        remote(most.at[da // 2], most_in.at[-da % 4, -dz % 4], rz_s.at[da, dz], rz_r.at[-da % 4, -dz % 4], place(da, 0, dz))
        for da, dz in near
    ]
    for copy in rz:
        copy.start()
    for copy in (*lz, *lp, ml, mm, *zs.values(), *copies):
        copy.wait_send()
    for group in B.values():
        for copy in group.values():
            copy.wait_send()
    most_in[0, 0] = most[0]
    for copy in rz:
        copy.wait_recv()
    quarter = iota((8, 128), 1) % 64 // 16
    sides = []
    for odd in range(2):
        side = jnp.full((8, 128), LOWEST, F32)
        for s in range(4):
            side = jnp.where(quarter == -s % 4, jnp.maximum(most_in[odd, s], most_in[odd + 2, s]), side)
        sides.append(side)
    final = jnp.maximum(sides[0], pltpu.roll(sides[1], 64, axis=1))
    final = jnp.max(final, axis=0, keepdims=True)[:, :DOC]
    l, k = iota((DOC, DOC), 0), iota((DOC, DOC), 1)
    column = jnp.max(jnp.where(l == k, final, LOWEST), axis=1, keepdims=True)
    takes = (k // 4 == l % 16) & (k % 4 == (z - l // 16 + 4) % 4)
    max_o[...] = jnp.max(jnp.where(takes, column, LOWEST), axis=0, keepdims=True) * SCALE
    for copy in rz:
        copy.wait_send()


def hand_on(embeddings, best, emb_o, max_o):
    emb_o[...] = embeddings[...]
    max_o[...] = best[...]


def step(features, doc_cluster, norm_gain, w_in, b_in, w_out, members, member_cluster, cluster_range):
    dma = pltpu.SemaphoreType.DMA
    anywhere = pl.BlockSpec(memory_space=pltpu.HBM)
    embeddings, best = pl.pallas_call(
        kernel,
        out_shape=(jax.ShapeDtypeStruct((DOC, D), BF16), jax.ShapeDtypeStruct((1, DOC), F32)),
        in_specs=[anywhere] * 9,
        out_specs=(pl.BlockSpec(memory_space=pltpu.VMEM), pl.BlockSpec(memory_space=pltpu.VMEM)),
        scratch_shapes=[
            pltpu.VMEM((DOC, D), BF16),
            pltpu.VMEM((1, DOC), jnp.int32),
            pltpu.VMEM((D,), F32),
            pltpu.VMEM((D, HID), BF16),
            pltpu.VMEM((1, HID), F32),
            pltpu.VMEM((HID, D), BF16),
            pltpu.VMEM((2, MEM, D), BF16),
            pltpu.VMEM((2, 8, 128), jnp.int32),
            pltpu.VMEM((2, CLUSTERS), jnp.int32),
            pltpu.VMEM((4, 16, D), BF16),
            pltpu.VMEM((4, 4, 4, 16, D), BF16),
            pltpu.VMEM((2 * MEM, 128), F32),
            pltpu.VMEM((4, 8, 128), F32),
            pltpu.VMEM((4, 4, 8, 128), F32),
            pltpu.VMEM((4, 2, 8, 128), F32),
            pltpu.VMEM((4, 2, 8, 128), F32),
            pltpu.VMEM((4, 2, 8, 128), F32),
            pltpu.VMEM((2, 8, 128), F32),
            pltpu.VMEM((4, 4, 8, 128), F32),
            dma((7,)), dma((2, CHUNKS)),
            dma((4, 4)), dma((4, 4)), dma((4,)), dma((4,)), dma, dma, dma, dma,
            dma((4, 4)), dma((4, 4)), dma((4, 4, 2)), dma((4, 4, 2)),
            dma((4,)), dma((4,)), dma((4, 4)), dma((4, 4)),
        ],
        compiler_params=pltpu.CompilerParams(
            collective_id=0, has_side_effects=True, vmem_limit_bytes=64 * 2**20
        ),
    )(
        features, doc_cluster.reshape(1, DOC), norm_gain, w_in, b_in.reshape(1, HID), w_out,
        members.reshape(MEM, D), member_cluster.reshape(8, 128), cluster_range.T,
    )
    embeddings, best = pl.pallas_call(
        hand_on,
        out_shape=(jax.ShapeDtypeStruct((DOC, D), BF16), jax.ShapeDtypeStruct((1, DOC), F32)),
        in_specs=[pl.BlockSpec(memory_space=pltpu.VMEM)] * 2,
        out_specs=(pl.BlockSpec(memory_space=pltpu.VMEM), pl.BlockSpec(memory_space=pltpu.VMEM)),
    )(embeddings, best)
    return embeddings, best.reshape(DOC)


def solution(mesh):
    placed = (
        P(("enc", "own"), None), P(("enc", "own")), P(), P(), P(), P(),
        P("own", "enc", None), P("own", "enc"), P(),
    )
    return jax.shard_map(
        step, mesh=mesh, in_specs=placed, out_specs=(P(("enc", "own"), None), P(("enc", "own"))), check_vma=False
    )
```

```python
import functools
import math

import jax
import jax.numpy as jnp
from jax import lax
from jax.experimental import pallas as pl
from jax.experimental.pallas import tpu as pltpu
from jax.sharding import PartitionSpec as P

MESH = pl.DeviceIdType.MESH
D = 768
HID = 3072
DOC = 64
MEM = 1024
CLUSTERS = 64
CHUNKS = 6
WINDOW = 3
STEP = HID // CHUNKS
SCALE = 1.0 / math.sqrt(D)
LOWEST = -1e30 / SCALE
F32 = jnp.float32
BF16 = jnp.bfloat16


def iota(shape, dim):
    return lax.broadcasted_iota(jnp.int32, shape, dim)


def kernel(
    feat_h, dcl_h, gain_h, w1_h, bin_h, w2_h, mem_h, mcl_h, cr_h,
    emb_o, max_o,
    feat, dcl, gain, w1, bin_, w2, mem, mlab, cr,
    sent, docs, memcol,
    lab_out, lab_z, lab_in, part, part_in,
    load_sem, w_sem,
    lz_s, lz_r, lp_s, lp_r, ml_s, ml_r, mm_s, mm_r,
    z_s, z_r, b_s, b_r, rp_s, rp_r,
):
    e = lax.axis_index("enc")
    o = lax.axis_index("own")
    x, c = e // 2, lax.rem(e, 2)
    z, y = o // 4, lax.rem(o, 4)
    a = x * (1 - c) + y * c
    b = y * (1 - c) + x * c

    def place(da, db, dz):
        pa, pb, pz = lax.rem(a + da, 4), lax.rem(b + db, 4), lax.rem(z + dz, 4)
        px = pa * (1 - c) + pb * c
        py = pb * (1 - c) + pa * c
        return (px * 2 + c, pz * 4 + py)

    other = (x * 2 + 1 - c, o)

    def remote(src, dst, ssem, rsem, where):
        return pltpu.make_async_remote_copy(
            src_ref=src, dst_ref=dst, send_sem=ssem, recv_sem=rsem,
            device_id=where, device_id_type=MESH,
        )

    def local(src, dst, sem):
        return pltpu.make_async_copy(src, dst, sem)

    small = [
        local(dcl_h, dcl, load_sem.at[0]),
        local(feat_h, feat, load_sem.at[1]),
        local(gain_h, gain, load_sem.at[2]),
        local(bin_h, bin_, load_sem.at[3]),
        local(cr_h, cr, load_sem.at[4]),
        local(mcl_h, mlab.at[0], load_sem.at[5]),
    ]
    for copy in small:
        copy.start()
    weights = []
    for j in range(CHUNKS):
        cols = pl.ds(j * STEP, STEP)
        weights.append((
            local(w1_h.at[:, cols], w1.at[:, cols], w_sem.at[0, j]),
            local(w2_h.at[cols], w2.at[cols], w_sem.at[1, j]),
        ))
        if j < WINDOW:
            weights[-1][0].start()
            weights[-1][1].start()
    members = local(mem_h, mem.at[0], load_sem.at[6])

    near = [(da, dz) for da in (0, 2, 1, 3) for dz in (2, 1, 3, 0) if (da, dz) != (0, 0)]
    barrier = pltpu.get_barrier_semaphore()
    pl.semaphore_signal(barrier, inc=1, device_id=other, device_id_type=MESH)
    for da in range(4):
        for db in range(4):
            for dz in range(4):
                if da or db or dz:
                    pl.semaphore_signal(barrier, inc=1, device_id=place(da, db, dz), device_id_type=MESH)

    small[1].wait()
    small[2].wait()
    r, k = iota((DOC, DOC), 0), iota((DOC, DOC), 1)
    order = jnp.where((k % 4 == (z + r // 16) % 4) & (k // 4 == r % 16), 1.0, 0.0).astype(BF16)
    inputs = jnp.dot(order, feat[...], preferred_element_type=F32)
    center = inputs - jnp.mean(inputs, axis=1, keepdims=True)
    spread = jnp.mean(center * center, axis=1, keepdims=True)
    normed = (center * lax.rsqrt(spread + 1e-05) * gain[...].reshape(1, D)).astype(BF16)
    small[3].wait()

    low = iota((8, 128), 1) < 64
    lp = [remote(lab_in.at[0], lab_in.at[4 - db], lp_s.at[db], lp_r.at[4 - db], place(0, db, 0)) for db in (1, 2, 3)]
    mm = remote(mem_h, mem.at[1], mm_s, mm_r, other)

    small[0].wait()
    k, lane = iota((DOC, 512), 0), iota((DOC, 512), 1)
    d, l = lane // 128, lane % 64
    hit = (k % 4 == (z + d) % 4) & (l // 16 == (4 - d) % 4) & (l % 16 == k // 4)
    spots = jnp.where(hit, 1.0, 0.0).astype(BF16)
    labels = jnp.broadcast_to(dcl[...].astype(F32), (8, DOC)).astype(BF16)
    spread = jnp.dot(labels, spots, preferred_element_type=F32)
    lab_z[0, 0] = spread[:, :128]
    for d in range(4):
        lab_out[d] = spread[:, d * 128 : (d + 1) * 128]

    lz = [
        remote(lab_out.at[dz], lab_z.at[-da % 4, -dz % 4], lz_s.at[da, dz], lz_r.at[-da % 4, -dz % 4], place(da, 0, dz))
        for da, dz in near
    ]
    small[5].wait()
    ml = remote(mlab.at[0], mlab.at[1], ml_s, ml_r, other)

    output = inputs
    for j in range(CHUNKS):
        weights[j][0].wait()
        pre = jnp.dot(normed, w1[:, j * STEP : (j + 1) * STEP], preferred_element_type=F32)
        hidden = jax.nn.gelu(pre + bin_[:, j * STEP : (j + 1) * STEP], approximate=True).astype(BF16)
        weights[j][1].wait()
        output = output + jnp.dot(hidden, w2[j * STEP : (j + 1) * STEP], preferred_element_type=F32)
        if j + WINDOW < CHUNKS:
            weights[j + WINDOW][0].start()
            weights[j + WINDOW][1].start()
        if j == 2:
            pl.semaphore_wait(barrier, 64)
            for copy in lz:
                copy.start()
            ml.start()
        if j == 3:
            members.start()
            mm.start()
    found = (output * lax.rsqrt(jnp.mean(output * output, axis=1, keepdims=True) + 1e-06)).astype(BF16)
    sent[...] = found.reshape(4, 16, D)
    docs[0, 0, 0] = found[:16]

    zs = {
        (-da % 4, -dz % 4): remote(
            sent.at[dz], docs.at[0, -da % 4, -dz % 4], z_s.at[da, dz], z_r.at[-da % 4, -dz % 4], place(da, 0, dz)
        )
        for da, dz in near
    }
    for copy in zs.values():
        copy.start()

    k, r = iota((DOC, DOC), 0), iota((DOC, DOC), 1)
    back = jnp.where((k % 4 == (z + r // 16) % 4) & (k // 4 == r % 16), 1.0, 0.0).astype(BF16)
    emb_o[...] = jnp.dot(back, found, preferred_element_type=F32).astype(BF16)

    B = {}

    def halves(dst, src, sem_s, sem_r, where, order):
        return {h: remote(src.at[pl.ds(2 * h, 2)], dst.at[pl.ds(2 * h, 2)], sem_s.at[h], sem_r.at[h], where) for h in order}

    for da in range(4):
        B[da, 3] = halves(docs.at[3, da], docs.at[0, da], b_s.at[da, 3], b_r.at[da, 3], place(0, 1, 0), (0, 1))
        B[da, 1] = halves(docs.at[1, da], docs.at[0, da], b_s.at[da, 1], b_r.at[da, 1], place(0, 3, 0), (1, 0))
        B[da, 2] = {
            0: remote(docs.at[3, da, pl.ds(0, 2)], docs.at[2, da, pl.ds(0, 2)], b_s.at[da, 2, 0], b_r.at[da, 2, 0], place(0, 1, 0)),
            1: remote(docs.at[1, da, pl.ds(2, 2)], docs.at[2, da, pl.ds(2, 2)], b_s.at[da, 2, 1], b_r.at[da, 2, 1], place(0, 3, 0)),
        }

    def send_b(da):
        for dz in range(4):
            if (da, dz) in zs:
                zs[da, dz].wait_recv()
        B[da, 3][0].start()
        B[da, 1][1].start()

    def send_rest(da):
        B[da, 3][1].start()
        B[da, 1][0].start()

    for copy in lz:
        copy.wait_recv()
    sums = [lab_z[da, 0] + lab_z[da, 1] + lab_z[da, 2] + lab_z[da, 3] for da in range(4)]
    lab_in[0, 0] = jnp.where(low, sums[0], sums[1])
    lab_in[0, 1] = jnp.where(low, sums[2], sums[3])
    for copy in lp:
        copy.start()

    small[4].wait()
    ml.wait_recv()
    number = iota((1, CLUSTERS), 1)
    inside = (cr[0:1] <= o) & (o <= cr[1:2])
    named = jnp.where(inside, number, -1).astype(F32)
    square = iota((CLUSTERS, CLUSTERS), 0) == iota((CLUSTERS, CLUSTERS), 1)
    table = jnp.dot(
        jnp.where(square, named, 0.0).astype(BF16), jnp.ones((CLUSTERS, 128), BF16), preferred_element_type=F32
    ).astype(BF16)
    eye = iota((128, 128), 0) == iota((128, 128), 1)
    ones = jnp.ones((128, 128), BF16)
    for half in range(2):
        for i in range(8):
            row = mlab[half, i : i + 1, :].astype(F32)
            col = jnp.dot(jnp.where(eye, row, 0.0).astype(BF16), ones, preferred_element_type=F32)
            onehot = jnp.where(col[:, :CLUSTERS] == iota((128, CLUSTERS), 1).astype(F32), 1.0, 0.0).astype(BF16)
            memcol[pl.ds((half * 8 + i) * 128, 128), :] = jnp.dot(onehot, table, preferred_element_type=F32)
    def pass_on(da):
        B[da, 3][0].wait_recv()
        B[da, 2][0].start()
        B[da, 1][1].wait_recv()
        B[da, 2][1].start()

    send_b(0)
    send_b(2)
    send_b(1)
    send_b(3)
    send_rest(0)
    send_rest(2)
    send_rest(1)
    send_rest(3)
    pass_on(0)
    pass_on(2)
    pass_on(1)
    pass_on(3)
    for copy in lp:
        copy.wait_recv()

    copies = []

    def match(db):
        block = docs[db].reshape(256, D)
        rows = [lab_in[db, h, :1] for h in range(2)]
        best = [jnp.full((8, 128), LOWEST, F32)] * 2
        for i in range(4):
            stock = mem[i // 2, pl.ds((i % 2) * 512, 512), :]
            score = lax.dot_general(stock, block, (((1,), (1,)), ((), ())), preferred_element_type=F32)
            column = memcol[pl.ds(i * 512, 512), :]
            for h in range(2):
                kept = jnp.where(column == rows[h], score[:, h * 128 : (h + 1) * 128], LOWEST)
                best[h] = jnp.maximum(best[h], jnp.max(kept.reshape(64, 8, 128), axis=0))
        for h in range(2):
            part[db, h] = jnp.max(best[h], axis=0, keepdims=True)
        for da in (2, 1, 3, 0):
            for dz in (2, 1, 3, 0):
                if da or db or dz:
                    copies.append(remote(
                        part.at[db, da // 2], part_in.at[-db % 4, -da % 4, -dz % 4],
                        rp_s.at[db, da, dz], rp_r.at[-db % 4, -da % 4, -dz % 4], place(da, db, dz),
                    ))
                    copies[-1].start()

    members.wait()
    mm.wait_recv()
    match(0)
    for da in range(4):
        B[da, 3][1].wait_recv()
    match(3)
    for da in range(4):
        B[da, 1][0].wait_recv()
    match(1)
    for da in range(4):
        B[da, 2][0].wait_recv()
        B[da, 2][1].wait_recv()
    match(2)

    part_in[0, 0, 0] = part[0, 0]
    for copy in (*lz, *lp, ml, mm, *zs.values()):
        copy.wait_send()
    for group in B.values():
        for copy in group.values():
            copy.wait_send()
    for copy in copies:
        copy.wait_recv()
    quarter = iota((1, 128), 1) % 64 // 16
    sides = []
    for odd in range(2):
        side = jnp.full((1, 128), LOWEST, F32)
        for s in range(4):
            most = part_in[0, odd, s]
            for q in range(1, 8):
                most = jnp.maximum(most, part_in[q // 2, odd + q % 2 * 2, s])
            side = jnp.where(quarter == -s % 4, most, side)
        sides.append(side)
    final = jnp.maximum(sides[0], pltpu.roll(sides[1], 64, axis=1))[:, :DOC]
    l, k = iota((DOC, DOC), 0), iota((DOC, DOC), 1)
    column = jnp.max(jnp.where(l == k, final, LOWEST), axis=1, keepdims=True)
    takes = (k // 4 == l % 16) & (k % 4 == (z - l // 16 + 4) % 4)
    max_o[...] = jnp.max(jnp.where(takes, column, LOWEST), axis=0, keepdims=True) * SCALE
    for copy in copies:
        copy.wait_send()


def hand_on(embeddings, best, emb_o, max_o):
    emb_o[...] = embeddings[...]
    max_o[...] = best[...]


def step(features, doc_cluster, norm_gain, w_in, b_in, w_out, members, member_cluster, cluster_range):
    dma = pltpu.SemaphoreType.DMA
    anywhere = pl.BlockSpec(memory_space=pltpu.HBM)
    embeddings, best = pl.pallas_call(
        kernel,
        out_shape=(jax.ShapeDtypeStruct((DOC, D), BF16), jax.ShapeDtypeStruct((1, DOC), F32)),
        in_specs=[anywhere] * 9,
        out_specs=(pl.BlockSpec(memory_space=pltpu.VMEM), pl.BlockSpec(memory_space=pltpu.VMEM)),
        scratch_shapes=[
            pltpu.VMEM((DOC, D), BF16),
            pltpu.VMEM((1, DOC), jnp.int32),
            pltpu.VMEM((D,), F32),
            pltpu.VMEM((D, HID), BF16),
            pltpu.VMEM((1, HID), F32),
            pltpu.VMEM((HID, D), BF16),
            pltpu.VMEM((2, MEM, D), BF16),
            pltpu.VMEM((2, 8, 128), jnp.int32),
            pltpu.VMEM((2, CLUSTERS), jnp.int32),
            pltpu.VMEM((4, 16, D), BF16),
            pltpu.VMEM((4, 4, 4, 16, D), BF16),
            pltpu.VMEM((2 * MEM, 128), F32),
            pltpu.VMEM((4, 8, 128), F32),
            pltpu.VMEM((4, 4, 8, 128), F32),
            pltpu.VMEM((4, 2, 8, 128), F32),
            pltpu.VMEM((4, 2, 1, 128), F32),
            pltpu.VMEM((4, 4, 4, 1, 128), F32),
            dma((7,)), dma((2, CHUNKS)),
            dma((4, 4)), dma((4, 4)), dma((4,)), dma((4,)), dma, dma, dma, dma,
            dma((4, 4)), dma((4, 4)), dma((4, 4, 2)), dma((4, 4, 2)),
            dma((4, 4, 4)), dma((4, 4, 4)),
        ],
        compiler_params=pltpu.CompilerParams(
            collective_id=0, has_side_effects=True, vmem_limit_bytes=64 * 2**20
        ),
    )(
        features, doc_cluster.reshape(1, DOC), norm_gain, w_in, b_in.reshape(1, HID), w_out,
        members.reshape(MEM, D), member_cluster.reshape(8, 128), cluster_range.T,
    )
    embeddings, best = pl.pallas_call(
        hand_on,
        out_shape=(jax.ShapeDtypeStruct((DOC, D), BF16), jax.ShapeDtypeStruct((1, DOC), F32)),
        in_specs=[pl.BlockSpec(memory_space=pltpu.VMEM)] * 2,
        out_specs=(pl.BlockSpec(memory_space=pltpu.VMEM), pl.BlockSpec(memory_space=pltpu.VMEM)),
    )(embeddings, best)
    return embeddings, best.reshape(DOC)


def solution(mesh):
    placed = (
        P(("enc", "own"), None), P(("enc", "own")), P(), P(), P(), P(),
        P("own", "enc", None), P("own", "enc"), P(),
    )
    return jax.shard_map(
        step, mesh=mesh, in_specs=placed, out_specs=(P(("enc", "own"), None), P(("enc", "own"))), check_vma=False
    )
```

```python
import functools
import math

import jax
import jax.numpy as jnp
from jax import lax
from jax.experimental import pallas as pl
from jax.experimental.pallas import tpu as pltpu
from jax.sharding import PartitionSpec as P

MESH = pl.DeviceIdType.MESH
D = 768
HID = 3072
DOC = 64
MEM = 1024
CLUSTERS = 64
CHUNKS = 6
WINDOW = 3
STEP = HID // CHUNKS
SCALE = 1.0 / math.sqrt(D)
LOWEST = -1e30 / SCALE
F32 = jnp.float32
BF16 = jnp.bfloat16


def iota(shape, dim):
    return lax.broadcasted_iota(jnp.int32, shape, dim)


def kernel(
    feat_h, dcl_h, gain_h, w1_h, bin_h, w2_h, mem_h, mcl_h, cr_h,
    emb_o, max_o,
    feat, dcl, gain, w1, bin_, w2, mem, mlab, cr,
    sent, docs, memcol,
    lab_out, lab_z, lab_in, part, part_in,
    load_sem, w_sem,
    lz_s, lz_r, lp_s, lp_r, ml_s, ml_r, mm_s, mm_r,
    z_s, z_r, b_s, b_r, rp_s, rp_r,
):
    e = lax.axis_index("enc")
    o = lax.axis_index("own")
    x, c = e // 2, lax.rem(e, 2)
    z, y = o // 4, lax.rem(o, 4)
    a = x * (1 - c) + y * c
    b = y * (1 - c) + x * c

    def place(da, db, dz):
        pa, pb, pz = lax.rem(a + da, 4), lax.rem(b + db, 4), lax.rem(z + dz, 4)
        px = pa * (1 - c) + pb * c
        py = pb * (1 - c) + pa * c
        return (px * 2 + c, pz * 4 + py)

    other = (x * 2 + 1 - c, o)

    def remote(src, dst, ssem, rsem, where):
        return pltpu.make_async_remote_copy(
            src_ref=src, dst_ref=dst, send_sem=ssem, recv_sem=rsem,
            device_id=where, device_id_type=MESH,
        )

    def local(src, dst, sem):
        return pltpu.make_async_copy(src, dst, sem)

    small = [
        local(dcl_h, dcl, load_sem.at[0]),
        local(feat_h, feat, load_sem.at[1]),
        local(gain_h, gain, load_sem.at[2]),
        local(bin_h, bin_, load_sem.at[3]),
        local(cr_h, cr, load_sem.at[4]),
        local(mcl_h, mlab.at[0], load_sem.at[5]),
    ]
    for copy in small:
        copy.start()
    weights = []
    for j in range(CHUNKS):
        cols = pl.ds(j * STEP, STEP)
        weights.append((
            local(w1_h.at[:, cols], w1.at[:, cols], w_sem.at[0, j]),
            local(w2_h.at[cols], w2.at[cols], w_sem.at[1, j]),
        ))
        if j < WINDOW:
            weights[-1][0].start()
            weights[-1][1].start()
    members = local(mem_h, mem.at[0], load_sem.at[6])

    near = [(da, dz) for da in (0, 1, 3, 2) for dz in (2, 1, 3, 0) if (da, dz) != (0, 0)]
    barrier = pltpu.get_barrier_semaphore()
    pl.semaphore_signal(barrier, inc=1, device_id=other, device_id_type=MESH)
    for da in range(4):
        for db in range(4):
            for dz in range(4):
                if da or db or dz:
                    pl.semaphore_signal(barrier, inc=1, device_id=place(da, db, dz), device_id_type=MESH)

    small[1].wait()
    small[2].wait()
    r, k = iota((DOC, DOC), 0), iota((DOC, DOC), 1)
    order = jnp.where((k % 4 == (z + r // 16) % 4) & (k // 4 == r % 16), 1.0, 0.0).astype(BF16)
    inputs = jnp.dot(order, feat[...], preferred_element_type=F32)
    center = inputs - jnp.mean(inputs, axis=1, keepdims=True)
    spread = jnp.mean(center * center, axis=1, keepdims=True)
    normed = (center * lax.rsqrt(spread + 1e-05) * gain[...].reshape(1, D)).astype(BF16)
    small[3].wait()

    low = iota((8, 128), 1) < 64
    lp = [remote(lab_in.at[0], lab_in.at[4 - db], lp_s.at[db], lp_r.at[4 - db], place(0, db, 0)) for db in (1, 2, 3)]
    mm = remote(mem_h, mem.at[1], mm_s, mm_r, other)

    small[0].wait()
    k, lane = iota((DOC, 512), 0), iota((DOC, 512), 1)
    d, l = lane // 128, lane % 64
    hit = (k % 4 == (z + d) % 4) & (l // 16 == (4 - d) % 4) & (l % 16 == k // 4)
    spots = jnp.where(hit, 1.0, 0.0).astype(BF16)
    labels = jnp.broadcast_to(dcl[...].astype(F32), (8, DOC)).astype(BF16)
    spread = jnp.dot(labels, spots, preferred_element_type=F32)
    lab_z[0, 0] = spread[:, :128]
    for d in range(4):
        lab_out[d] = spread[:, d * 128 : (d + 1) * 128]

    lz = [
        remote(lab_out.at[dz], lab_z.at[-da % 4, -dz % 4], lz_s.at[da, dz], lz_r.at[-da % 4, -dz % 4], place(da, 0, dz))
        for da, dz in near
    ]
    small[5].wait()
    ml = remote(mlab.at[0], mlab.at[1], ml_s, ml_r, other)

    output = inputs
    for j in range(CHUNKS):
        weights[j][0].wait()
        pre = jnp.dot(normed, w1[:, j * STEP : (j + 1) * STEP], preferred_element_type=F32)
        hidden = jax.nn.gelu(pre + bin_[:, j * STEP : (j + 1) * STEP], approximate=True).astype(BF16)
        weights[j][1].wait()
        output = output + jnp.dot(hidden, w2[j * STEP : (j + 1) * STEP], preferred_element_type=F32)
        if j + WINDOW < CHUNKS:
            weights[j + WINDOW][0].start()
            weights[j + WINDOW][1].start()
        if j == 2:
            pl.semaphore_wait(barrier, 64)
            for copy in lz:
                copy.start()
            ml.start()
        if j == 3:
            members.start()
            mm.start()
    found = (output * lax.rsqrt(jnp.mean(output * output, axis=1, keepdims=True) + 1e-06)).astype(BF16)
    sent[...] = found.reshape(4, 16, D)
    docs[0, 0, 0] = found[:16]

    zs = {
        (-da % 4, -dz % 4): remote(
            sent.at[dz], docs.at[0, -da % 4, -dz % 4], z_s.at[da, dz], z_r.at[-da % 4, -dz % 4], place(da, 0, dz)
        )
        for da, dz in near
    }
    for copy in zs.values():
        copy.start()

    k, r = iota((DOC, DOC), 0), iota((DOC, DOC), 1)
    back = jnp.where((k % 4 == (z + r // 16) % 4) & (k // 4 == r % 16), 1.0, 0.0).astype(BF16)
    emb_o[...] = jnp.dot(back, found, preferred_element_type=F32).astype(BF16)

    B = {}

    def halves(dst, src, sem_s, sem_r, where, order):
        return {h: remote(src.at[pl.ds(2 * h, 2)], dst.at[pl.ds(2 * h, 2)], sem_s.at[h], sem_r.at[h], where) for h in order}

    for da in range(4):
        B[da, 3] = halves(docs.at[3, da], docs.at[0, da], b_s.at[da, 3], b_r.at[da, 3], place(0, 1, 0), (0, 1))
        B[da, 1] = halves(docs.at[1, da], docs.at[0, da], b_s.at[da, 1], b_r.at[da, 1], place(0, 3, 0), (1, 0))
        B[da, 2] = {
            0: remote(docs.at[3, da, pl.ds(0, 2)], docs.at[2, da, pl.ds(0, 2)], b_s.at[da, 2, 0], b_r.at[da, 2, 0], place(0, 1, 0)),
            1: remote(docs.at[1, da, pl.ds(2, 2)], docs.at[2, da, pl.ds(2, 2)], b_s.at[da, 2, 1], b_r.at[da, 2, 1], place(0, 3, 0)),
        }

    def send_b(da):
        for dz in range(4):
            if (da, dz) in zs:
                zs[da, dz].wait_recv()
        B[da, 3][0].start()
        B[da, 1][1].start()

    def send_rest(da):
        B[da, 3][1].start()
        B[da, 1][0].start()

    for copy in lz:
        copy.wait_recv()
    sums = [lab_z[da, 0] + lab_z[da, 1] + lab_z[da, 2] + lab_z[da, 3] for da in range(4)]
    lab_in[0, 0] = jnp.where(low, sums[0], sums[1])
    lab_in[0, 1] = jnp.where(low, sums[2], sums[3])
    for copy in lp:
        copy.start()

    small[4].wait()
    ml.wait_recv()
    number = iota((1, CLUSTERS), 1)
    inside = (cr[0:1] <= o) & (o <= cr[1:2])
    named = jnp.where(inside, number, -1).astype(F32)
    square = iota((CLUSTERS, CLUSTERS), 0) == iota((CLUSTERS, CLUSTERS), 1)
    table = jnp.dot(
        jnp.where(square, named, 0.0).astype(BF16), jnp.ones((CLUSTERS, 128), BF16), preferred_element_type=F32
    ).astype(BF16)
    eye = iota((128, 128), 0) == iota((128, 128), 1)
    ones = jnp.ones((128, 128), BF16)
    for half in range(2):
        for i in range(8):
            row = mlab[half, i : i + 1, :].astype(F32)
            col = jnp.dot(jnp.where(eye, row, 0.0).astype(BF16), ones, preferred_element_type=F32)
            onehot = jnp.where(col[:, :CLUSTERS] == iota((128, CLUSTERS), 1).astype(F32), 1.0, 0.0).astype(BF16)
            memcol[pl.ds((half * 8 + i) * 128, 128), :] = jnp.dot(onehot, table, preferred_element_type=F32)
    def pass_on(da):
        B[da, 3][0].wait_recv()
        B[da, 2][0].start()
        B[da, 1][1].wait_recv()
        B[da, 2][1].start()

    send_b(0)
    send_b(1)
    send_b(3)
    send_b(2)
    send_rest(0)
    send_rest(2)
    send_rest(1)
    send_rest(3)
    pass_on(0)
    pass_on(2)
    pass_on(1)
    pass_on(3)
    for copy in lp:
        copy.wait_recv()

    copies = []

    def match(db):
        block = docs[db].reshape(256, D)
        rows = [lab_in[db, h, :1] for h in range(2)]
        best = [jnp.full((8, 128), LOWEST, F32)] * 2
        for i in range(4):
            stock = mem[i // 2, pl.ds((i % 2) * 512, 512), :]
            score = lax.dot_general(stock, block, (((1,), (1,)), ((), ())), preferred_element_type=F32)
            column = memcol[pl.ds(i * 512, 512), :]
            for h in range(2):
                kept = jnp.where(column == rows[h], score[:, h * 128 : (h + 1) * 128], LOWEST)
                best[h] = jnp.maximum(best[h], jnp.max(kept.reshape(64, 8, 128), axis=0))
        for h in range(2):
            part[db, h] = jnp.max(best[h], axis=0, keepdims=True)
        for da in (2, 1, 3, 0):
            for dz in (2, 1, 3, 0):
                if da or db or dz:
                    copies.append(remote(
                        part.at[db, da // 2], part_in.at[-db % 4, -da % 4, -dz % 4],
                        rp_s.at[db, da, dz], rp_r.at[-db % 4, -da % 4, -dz % 4], place(da, db, dz),
                    ))
                    copies[-1].start()

    members.wait()
    mm.wait_recv()
    match(0)
    for da in range(4):
        B[da, 3][1].wait_recv()
    match(3)
    for da in range(4):
        B[da, 1][0].wait_recv()
    match(1)
    for da in range(4):
        B[da, 2][0].wait_recv()
        B[da, 2][1].wait_recv()
    match(2)

    part_in[0, 0, 0] = part[0, 0]
    for copy in (*lz, *lp, ml, mm, *zs.values()):
        copy.wait_send()
    for group in B.values():
        for copy in group.values():
            copy.wait_send()
    for copy in copies:
        copy.wait_recv()
    quarter = iota((1, 128), 1) % 64 // 16
    sides = []
    for odd in range(2):
        side = jnp.full((1, 128), LOWEST, F32)
        for s in range(4):
            most = part_in[0, odd, s]
            for q in range(1, 8):
                most = jnp.maximum(most, part_in[q // 2, odd + q % 2 * 2, s])
            side = jnp.where(quarter == -s % 4, most, side)
        sides.append(side)
    final = jnp.maximum(sides[0], pltpu.roll(sides[1], 64, axis=1))[:, :DOC]
    l, k = iota((DOC, DOC), 0), iota((DOC, DOC), 1)
    column = jnp.max(jnp.where(l == k, final, LOWEST), axis=1, keepdims=True)
    takes = (k // 4 == l % 16) & (k % 4 == (z - l // 16 + 4) % 4)
    max_o[...] = jnp.max(jnp.where(takes, column, LOWEST), axis=0, keepdims=True) * SCALE
    for copy in copies:
        copy.wait_send()


def hand_on(embeddings, best, emb_o, max_o):
    emb_o[...] = embeddings[...]
    max_o[...] = best[...]


def step(features, doc_cluster, norm_gain, w_in, b_in, w_out, members, member_cluster, cluster_range):
    dma = pltpu.SemaphoreType.DMA
    anywhere = pl.BlockSpec(memory_space=pltpu.HBM)
    embeddings, best = pl.pallas_call(
        kernel,
        out_shape=(jax.ShapeDtypeStruct((DOC, D), BF16), jax.ShapeDtypeStruct((1, DOC), F32)),
        in_specs=[anywhere] * 9,
        out_specs=(pl.BlockSpec(memory_space=pltpu.VMEM), pl.BlockSpec(memory_space=pltpu.VMEM)),
        scratch_shapes=[
            pltpu.VMEM((DOC, D), BF16),
            pltpu.VMEM((1, DOC), jnp.int32),
            pltpu.VMEM((D,), F32),
            pltpu.VMEM((D, HID), BF16),
            pltpu.VMEM((1, HID), F32),
            pltpu.VMEM((HID, D), BF16),
            pltpu.VMEM((2, MEM, D), BF16),
            pltpu.VMEM((2, 8, 128), jnp.int32),
            pltpu.VMEM((2, CLUSTERS), jnp.int32),
            pltpu.VMEM((4, 16, D), BF16),
            pltpu.VMEM((4, 4, 4, 16, D), BF16),
            pltpu.VMEM((2 * MEM, 128), F32),
            pltpu.VMEM((4, 8, 128), F32),
            pltpu.VMEM((4, 4, 8, 128), F32),
            pltpu.VMEM((4, 2, 8, 128), F32),
            pltpu.VMEM((4, 2, 1, 128), F32),
            pltpu.VMEM((4, 4, 4, 1, 128), F32),
            dma((7,)), dma((2, CHUNKS)),
            dma((4, 4)), dma((4, 4)), dma((4,)), dma((4,)), dma, dma, dma, dma,
            dma((4, 4)), dma((4, 4)), dma((4, 4, 2)), dma((4, 4, 2)),
            dma((4, 4, 4)), dma((4, 4, 4)),
        ],
        compiler_params=pltpu.CompilerParams(
            collective_id=0, has_side_effects=True, vmem_limit_bytes=64 * 2**20
        ),
    )(
        features, doc_cluster.reshape(1, DOC), norm_gain, w_in, b_in.reshape(1, HID), w_out,
        members.reshape(MEM, D), member_cluster.reshape(8, 128), cluster_range.T,
    )
    embeddings, best = pl.pallas_call(
        hand_on,
        out_shape=(jax.ShapeDtypeStruct((DOC, D), BF16), jax.ShapeDtypeStruct((1, DOC), F32)),
        in_specs=[pl.BlockSpec(memory_space=pltpu.VMEM)] * 2,
        out_specs=(pl.BlockSpec(memory_space=pltpu.VMEM), pl.BlockSpec(memory_space=pltpu.VMEM)),
    )(embeddings, best)
    return embeddings, best.reshape(DOC)


def solution(mesh):
    placed = (
        P(("enc", "own"), None), P(("enc", "own")), P(), P(), P(), P(),
        P("own", "enc", None), P("own", "enc"), P(),
    )
    return jax.shard_map(
        step, mesh=mesh, in_specs=placed, out_specs=(P(("enc", "own"), None), P(("enc", "own"))), check_vma=False
    )
```
